32 devices in a mesh: section: 8 (over y, x, core), tp: 4 (over z).
Axes of the slice: x: 2, y: 2, z: 4, core: 2. Of those that a mesh axis runs over, the one named last changes fastest.
Arguments:
- hidden_in: bfloat16 [8, 256, 8192], P('section', None, 'tp'), may hold values from -6 to 6
- gain: bfloat16 [8, 8192], P('section', 'tp'), may hold values from 0.5 to 1.5
- w_kv: bfloat16 [8, 8192, 2048], P('section', 'tp'), may hold values from -0.125 to 0.125
- g_kv: bfloat16 [8, 256, 2048], P('section', None, 'tp'), may hold values from -6 to 6
- attn: bfloat16 [8, 256, 8192], P('section', None, 'tp'), may hold values from -6 to 6
- top_grad: bfloat16 [256, 8192], P(None, 'tp'), may hold values from -6 to 6
- pin_kv: bfloat16 [8, 8192, 64], P('section', 'tp'), may hold values from -0.0625 to 0.0625
- pout_kv: bfloat16 [8, 2048, 64], P('section', 'tp'), may hold values from -0.125 to 0.125
- pin_o: bfloat16 [8, 8192, 64], P('section', 'tp'), may hold values from -0.0625 to 0.0625
- pout_o: bfloat16 [8, 8192, 64], P('section', 'tp'), may hold values from -0.0625 to 0.0625
- queries: bfloat16 [8, 2, 256, 4096], P('section', None, None, 'tp'), may hold values from -0.001953125 to 0.001953125
- lengths: int32 [2, 4], replicated, may hold values from 1 to 64, 128 in all within a row
Outputs:
- scores: float32 [8, 256], replicated
The draws below stay inside these ranges and needn't reach their ends.
Inputs may be any that keep to these rules, and one draw needn't show every extreme that they name: Each row holds 4 lengths that sum to 128; some length equals the most.
All inputs are finite; a program needn't handle non-finite values.
Results may differ from the reference program's by a relative error of at most 0.0041.
Values may be sent and summed in bfloat16 or wider, within the bound.
A program may use at most 128 MiB of HBM per device.

```python
import math
import jax
import jax.numpy as jnp
import numpy as np
from jax import lax

D = 8192
KVW = 2048
R = 64
MB_TOK = 128
EPM = 4
MB = 2
NQ = 256
SECTIONS = 8
TOK = 256


def block_scale(key, extent, shards, smallest, largest):
    def one(dim, shards_of):
        steps = jax.random.uniform(jax.random.fold_in(jax.random.fold_in(key, 6), dim), (shards_of,), jnp.float32, smallest / len(shards), largest / len(shards))
        return jnp.repeat(jnp.exp(steps), extent[dim] // shards_of).reshape((-1,) + (1,) * (len(extent) - dim - 1))

    level = one(*shards[0])
    for cut in shards[1:]:
        level = level * one(*cut)
    return level


def profile(amount, total, most, slope):
    loads = [(1 << 20) // math.isqrt(standing ** slope) + 1 for standing in range(2, amount + 1)]
    spare, counts = total - most - (amount - 1), [1] * (amount - 1)
    while spare > 0:
        candidates = [i for i in range(amount - 1) if counts[i] < most]
        mass, remaining = sum([loads[i] for i in candidates]), spare
        for i in candidates:
            addition = min(most - counts[i], max(1, remaining * loads[i] // mass), spare)
            counts[i] = counts[i] + addition
            spare = spare - addition
    return np.array([most] + counts)


def ragged(rng, count, total, reach, slope):
    if count == 2:
        one = jax.random.randint(rng, (), max(1, total - reach), min(reach, total - 1) + 1)
        return jnp.stack([one, total - one])
    tallies = jnp.asarray(profile(count, total, reach, slope), jnp.int32)
    pairs = (count - 1) // 2
    giver, sink = tallies[1:1 + 2 * pairs:2], tallies[2:2 + 2 * pairs:2]
    margin = jnp.minimum(giver - 1, reach - sink)
    moved = jax.random.randint(jax.random.fold_in(rng, 1), (pairs,), 0, 1 << 20) % (margin + 1)
    tallies = tallies.at[1:1 + 2 * pairs:2].set(giver - moved).at[2:2 + 2 * pairs:2].set(sink + moved)
    return tallies[jax.random.permutation(jax.random.fold_in(rng, 2), count)]


def gaussian(stream_key, dims, deviation, bound, cuts=(), kind=jnp.bfloat16):
    values = jax.random.normal(stream_key, dims, jnp.float32) * deviation
    if len(cuts) > 0:
        values = block_scale(stream_key, dims, cuts, -0.22, 0.18) * values
    return jnp.clip(values, min=-bound, max=bound).astype(kind)


def setup_inputs(seed: int = 0) -> dict:
    streams_of = jax.random.split(jax.random.key(seed), 13)
    return {
        "hidden_in": gaussian(streams_of[0], (SECTIONS, TOK, D), 1.0, 6.0, ((0, 8), (2, 4))),
        "gain": jnp.clip(1.0 + 0.1 * jax.random.normal(streams_of[1], (SECTIONS, D), jnp.float32), 0.5, 1.5).astype(jnp.bfloat16),
        "w_kv": gaussian(streams_of[2], (SECTIONS, D, KVW), KVW ** -0.5, 0.125, ((0, 8), (1, 4))),
        "g_kv": gaussian(streams_of[3], (SECTIONS, TOK, KVW), 1.0, 6.0, ((0, 8), (2, 4))),
        "attn": gaussian(streams_of[4], (SECTIONS, TOK, D), 1.0, 6.0, ((0, 8), (2, 4))),
        "top_grad": gaussian(streams_of[5], (TOK, D), 1.0, 6.0, ((1, 4),)),
        "pin_kv": gaussian(streams_of[6], (SECTIONS, D, R), D ** -0.5, 0.0625, ((0, 8), (1, 4))),
        "pout_kv": gaussian(streams_of[7], (SECTIONS, KVW, R), KVW ** -0.5, 0.125, ((0, 8), (1, 4))),
        "pin_o": gaussian(streams_of[8], (SECTIONS, D, R), D ** -0.5, 0.0625, ((0, 8), (1, 4))),
        "pout_o": gaussian(streams_of[9], (SECTIONS, D, R), D ** -0.5, 0.0625, ((0, 8), (1, 4))),
        "queries": gaussian(streams_of[10], (SECTIONS, 2, NQ, R * R), (256 * R * R * SECTIONS) ** -0.5, 0.001953125, ((0, 8), (3, 4))),
        "lengths": jax.vmap(lambda own: ragged(own, EPM, MB_TOK, MB_TOK // 2, 2))(jax.random.split(streams_of[11], MB)).reshape((MB, EPM)).astype(jnp.int32),
    }


EPSILON = 1e-05

def example_masks(lengths):
    end_points = jnp.cumsum(lengths, axis=1)
    starts = end_points - lengths
    position = lax.broadcasted_iota(jnp.int32, (1, 1, MB_TOK), 2)
    inside = (position >= starts[:, :, None]) & (position < end_points[:, :, None])
    return inside.astype(jnp.float32)

def example_grads(example_mask, left_rows, right_rows):
    batches = example_mask.shape[0]
    left_side = left_rows.reshape(batches, MB_TOK, left_rows.shape[-1])
    right_side = right_rows.reshape(batches, MB_TOK, right_rows.shape[-1])
    weighted = example_mask[:, :, :, None] * left_side[:, None]
    outer_sums = jnp.einsum('meti,mtj->meij', weighted, right_side, precision=lax.Precision.HIGHEST)
    return outer_sums.reshape(-1, left_rows.shape[-1] * right_rows.shape[-1]).astype(jnp.bfloat16)

def score_terms(grad_rows, query_rows):
    return lax.dot_general(grad_rows, query_rows, (((1,), (1,)), ((), ())), preferred_element_type=jnp.float32)

def reference(hidden_in, gain, w_kv, g_kv, attn, top_grad, pin_kv, pout_kv, pin_o, pout_o, queries, lengths):
    example_mask = example_masks(lengths)

    def local_terms(operands):
        block_in, block_gain, weights, cotangent, projector = operands
        inputs = block_in.astype(jnp.float32)
        gains = block_gain.astype(jnp.float32)
        scaled = inputs * gains
        projected_in = jnp.dot(scaled.astype(jnp.bfloat16), projector, preferred_element_type=jnp.float32)
        inverse_rms = lax.rsqrt(lax.optimization_barrier(jnp.sum(inputs * inputs, axis=1)) / D + EPSILON)
        grad_norm_out = lax.dot_general(cotangent, weights, (((1,), (1,)), ((), ())), preferred_element_type=jnp.float32)
        dot_sums = lax.optimization_barrier(jnp.sum(scaled * grad_norm_out, axis=1))
        branch = inverse_rms[:, None] * gains * grad_norm_out - inputs * (inverse_rms ** 3 / D * dot_sums)[:, None]
        return (branch, inverse_rms[:, None] * projected_in)
    branches, key_inputs = lax.map(local_terms, (hidden_in, gain, w_kv, g_kv, pin_kv))

    def carry_down(running, branch):
        return (running + branch, running)
    _, residuals = lax.scan(carry_down, top_grad.astype(jnp.float32), branches, reverse=True)

    def block_scores(operands):
        key_rows, cotangent, out_proj, attn_rows, attn_proj, residual, resid_proj, query_block = operands
        value_proj = jnp.dot(cotangent, out_proj, preferred_element_type=jnp.float32)
        attn_in = jnp.dot(attn_rows, attn_proj, preferred_element_type=jnp.float32)
        output_proj = jnp.dot(residual.astype(jnp.bfloat16), resid_proj, preferred_element_type=jnp.float32)
        kv_grads = example_grads(example_mask, key_rows, value_proj)
        out_grads = example_grads(example_mask, attn_in, output_proj)
        return score_terms(kv_grads, query_block[0]) + score_terms(out_grads, query_block[1])
    partials = lax.map(block_scores, (key_inputs, g_kv, pout_kv, attn, pin_o, residuals, pout_o, queries))
    return lax.optimization_barrier(jnp.sum(partials, axis=0))
```

```python
import functools

import jax
import jax.numpy as jnp
from jax import lax
from jax.experimental import pallas as pl
from jax.experimental.pallas import tpu as pltpu
from jax.sharding import PartitionSpec as P

EPSILON = 1e-05
MESH = pl.DeviceIdType.MESH
NT = (((1,), (1,)), ((), ()))


def dot_nt(a, b):
    return lax.dot_general(a, b, NT, preferred_element_type=jnp.float32)


def fold(x):
    total = x[:, :128]
    for first in range(128, x.shape[1], 128):
        total = total + x[:, first:first + 128]
    return total


def as_row(x):
    return jnp.sum(x.T, axis=0, keepdims=True)


def kernel(
    S, n,
    hid_h, gain_h, w_h, g_h, att_h, top_h, pik_h, pok_h, pio_h, poo_h, q_h, len_s,
    out_ref,
    hid, gain, w, g, att, top, pik, pok, pio, pout, q,
    da, e, a_t, b_t, p_send, p_recv,
    sq_send, sq_recv, dt_send, dt_recv, u_send, u_recv, vk_send, vk_recv,
    vo_send, vo_recv, vtop, fs_send, fs_recv, ft_send, ft_recv,
    loc, w_sem, g_up, g_dn, g_rs, po_ss, po_sib, po_fw, po_rs,
    sq_ss, sq_rs, dt_ss, dt_rs, u_ss, u_rs, vk_ss, vk_rs, vo_ss, vo_rs,
    p_ss, p_rs, fs_ss, fs_rs, ft_ss, ft_rs,
):
    sec, z = lax.axis_index("section"), lax.axis_index("tp")
    chip, core = sec // 2, sec % 2
    sib = 2 * chip + 1 - core
    T, d = hid.shape
    kc = g.shape[2]
    R = pik.shape[0]
    ri = R // n
    D = d * n
    half = T // 2
    tile = min(d, 512)
    tiles = d // tile

    def remote(src, dst, ss, rs, s_, z_):
        return pltpu.make_async_remote_copy(
            src_ref=src, dst_ref=dst, send_sem=ss, recv_sem=rs,
            device_id={"section": s_, "tp": z_}, device_id_type=MESH,
        )

    def tp_peers():
        return [lax.rem(z + o, n) for o in range(1, n)]

    g_load = pltpu.make_async_copy(g_h, g.at[z], loc.at[0])
    po_load = pltpu.make_async_copy(poo_h, pout.at[sec], loc.at[1])
    g_load.start()
    po_load.start()
    rest = [
        pltpu.make_async_copy(src, dst, loc.at[2 + i])
        for i, (src, dst) in enumerate(
            [(hid_h, hid), (gain_h, gain), (pik_h, pik), (att_h, att), (pio_h, pio),
             (pok_h, pok), (top_h, top), (q_h, q)]
        )
    ]
    hid_l, gain_l, pik_l, att_l, pio_l, pok_l, top_l, q_l = rest
    for c in rest[:6]:
        c.start()

    def w_load(ch):
        return pltpu.make_async_copy(
            w_h.at[:, pl.ds(pl.multiple_of(ch * kc, 128), kc)], w.at[ch], w_sem.at[ch]
        )

    w_load(z).start()
    for peer in tp_peers():
        w_load(peer).start()
    top_l.start()
    q_l.start()

    barrier = pltpu.get_barrier_semaphore()
    for peer in tp_peers():
        pl.semaphore_signal(barrier, inc=1, device_id={"section": sec, "tp": peer}, device_id_type=MESH)

    def greet(o, carry):
        pl.semaphore_signal(
            barrier, inc=1, device_id={"section": lax.rem(sec + o, S), "tp": z}, device_id_type=MESH
        )
        return carry

    lax.fori_loop(1, S, greet, 0)
    pl.semaphore_wait(barrier, n - 1 + S - 1)

    def g_copy(ch, h, hf, up):
        part = g.at[ch, pl.ds(hf * half, half)]
        sems = g_up if up else g_dn
        return remote(part, part, sems.at[h, hf], g_rs.at[ch, hf], sec, z + 1 if up else z - 1)

    g_load.wait()
    for hf in range(2):
        @pl.when(z < n - 1)
        def _():
            g_copy(z, 0, hf, True).start()

        @pl.when(z > 0)
        def _():
            g_copy(z, 0, hf, False).start()

    po_load.wait()

    def po_copy(c_):
        return remote(pout.at[sec], pout.at[sec], po_ss.at[c_], po_rs.at[sec], 2 * c_ + core, z)

    def po_sibling():
        return remote(pout.at[sec], pout.at[sec], po_sib, po_rs.at[sec], sib, z)

    def po_forward(c_):
        s_ = 2 * c_ + core
        return remote(pout.at[s_], pout.at[s_], po_fw.at[c_], po_rs.at[s_], sib, z)

    def each(lo, hi, act):
        def body(i, carry):
            act(i)
            return carry
        lax.fori_loop(lo, hi, body, 0)

    each(chip + 1, S // 2, lambda c_: po_copy(c_).start())

    @pl.when(core == 0)
    def _():
        po_sibling().start()

    hid_l.wait()
    gain_l.wait()

    def cut(i):
        return pl.ds(pl.multiple_of(i * tile, 128), tile)

    def squares(i, total):
        x = hid[:, cut(i)].astype(jnp.float32)
        e[:, cut(i)] = (x * gain[:, cut(i)].astype(jnp.float32)).astype(jnp.bfloat16)
        return total + fold(x * x)

    sq_mine = as_row(lax.fori_loop(0, tiles, squares, jnp.zeros((T, 128), jnp.float32)))

    def to_peers(send, recv, ss, rs):
        return [remote(send, recv.at[z], ss.at[peer], rs.at[z], sec, peer) for peer in tp_peers()]

    def from_peers(recv, ss, rs):
        for peer in tp_peers():
            remote(recv.at[peer], recv.at[peer], ss.at[peer], rs.at[peer], sec, peer).wait_recv()

    sq_send[...] = sq_mine
    sq_out = to_peers(sq_send, sq_recv, sq_ss, sq_rs)
    for c in sq_out:
        c.start()

    pik_l.wait()
    uk = dot_nt(pik[...], e[...])
    pok_l.wait()
    vk = dot_nt(pok[...], g[z])
    att_l.wait()
    pio_l.wait()
    uo = dot_nt(pio[...], att[...])
    for j in range(n):
        u_send[j, 0] = uk[j * ri:(j + 1) * ri]
        u_send[j, 1] = uo[j * ri:(j + 1) * ri]
    vk_send[...] = vk.astype(jnp.bfloat16)
    vkv = vk

    def gather_product(ch, first=False):
        def body(i, carry):
            rows = pl.ds(pl.multiple_of(i * tile, 128), tile)
            part = dot_nt(g[ch], w[ch, rows, :])
            if first:
                da[:, cut(i)] = part
            else:
                da[:, cut(i)] += part
            return carry
        w_load(ch).wait()
        lax.fori_loop(0, tiles, body, 0)

    gather_product(z, first=True)
    top_l.wait()
    vtop[...] = dot_nt(pout[sec], top[...])

    def b_part(group):
        width = min(S, 4)

        def body(i, carry):
            rows = pl.ds(pl.multiple_of(i * width * R, 128), width * R)
            group(rows, pout[pl.ds(i * width, width)].reshape(width * R, d))
            return carry
        lax.fori_loop(0, S // width, body, 0)

    def project_inputs(rows, po):
        b_t[rows, :] = dot_nt(po, hid[...])

    def project_grads(rows, po):
        a_t[rows, :] = dot_nt(po, e[...])

    for h in range(1, n):
        if h == n - 1:
            def pass_on(c_):
                po_copy_in(2 * c_ + core)
                po_forward(c_).start()

            def po_copy_in(s_):
                remote(pout.at[s_], pout.at[s_], po_sib, po_rs.at[s_], sib, z).wait_recv()

            each(0, chip, pass_on)
            each(0, chip, lambda c_: po_copy_in(2 * c_ + 1 - core))

            @pl.when(core == 1)
            def _():
                po_copy_in(sib)

            b_part(project_inputs)
        for hf in range(2):
            @pl.when(z >= h)
            def _():
                g_copy(z - h, h, hf, True).wait_recv()

                @pl.when(z < n - 1)
                def _():
                    g_copy(z - h, h, hf, True).start()

            @pl.when(z + h < n)
            def _():
                g_copy(z + h, h, hf, False).wait_recv()

                @pl.when(z > 0)
                def _():
                    g_copy(z + h, h, hf, False).start()

        @pl.when(z >= h)
        def _():
            gather_product(z - h)

        @pl.when(z + h < n)
        def _():
            gather_product(z + h)

    def weigh(i, total):
        part = da[:, cut(i)] * gain[:, cut(i)].astype(jnp.float32)
        e[:, cut(i)] = part.astype(jnp.bfloat16)
        return total + fold(part * hid[:, cut(i)].astype(jnp.float32))

    dt_mine = as_row(lax.fori_loop(0, tiles, weigh, jnp.zeros((T, 128), jnp.float32)))
    dt_send[...] = dt_mine
    dt_out = to_peers(dt_send, dt_recv, dt_ss, dt_rs)
    for c in dt_out:
        c.start()
    u_out = [remote(u_send.at[p], u_recv.at[z], u_ss.at[p], u_rs.at[z], sec, p) for p in tp_peers()]
    vk_out = to_peers(vk_send, vk_recv, vk_ss, vk_rs)
    for c in u_out + vk_out:
        c.start()

    b_part(project_grads)
    from_peers(sq_recv, sq_ss, sq_rs)
    sq_total = sq_mine
    for p in tp_peers():
        sq_total = sq_total + sq_recv[p]
    inv = lax.rsqrt(sq_total / D + EPSILON)
    from_peers(dt_recv, dt_ss, dt_rs)
    dt_total = dt_mine
    for p in tp_peers():
        dt_total = dt_total + dt_recv[p]
    coef = inv * inv * inv / D * dt_total

    def p_copy(s_):
        return remote(p_send.at[s_], p_recv.at[sec], p_ss.at[s_], p_rs.at[sec], s_, z)

    def p_make(s_):
        rows = pl.ds(pl.multiple_of(s_ * R, R), R)
        p_send[s_] = (inv * a_t[rows, :] - coef * b_t[rows, :]).astype(jnp.bfloat16)
        p_copy(s_).start()

    each(0, sec, p_make)

    batches, per = len_s.shape
    E = batches * per
    row = lax.broadcasted_iota(jnp.int32, (E, T), 0)
    token = lax.broadcasted_iota(jnp.int32, (E, T), 1)
    starts = jnp.zeros((E, T), jnp.int32)
    ends = jnp.zeros((E, T), jnp.int32)
    for m in range(batches):
        at = jnp.int32(m * (T // batches))
        for k in range(per):
            starts = jnp.where(row == m * per + k, at, starts)
            at = at + len_s[m, k]
            ends = jnp.where(row == m * per + k, at, ends)
    mask = jnp.where((token >= starts) & (token < ends), 1.0, 0.0).astype(jnp.float32)

    def layer_scores(u, v_t, layer):
        left = jnp.concatenate([mask * u[i:i + 1] for i in range(ri)], axis=0)
        grads = lax.dot_general(
            left, jnp.concatenate([v_t, v_t], axis=0), NT,
            precision=lax.Precision.HIGHEST, preferred_element_type=jnp.float32,
        )
        low = lax.broadcasted_iota(jnp.int32, (E, 2 * R), 1) < R
        pieces = [
            jnp.where(low, grads[i * E:(i + 1) * E], grads[(i + 1) * E:(i + 2) * E])
            for i in range(0, ri, 2)
        ]
        flat = jnp.concatenate(pieces, axis=1) if len(pieces) > 1 else pieces[0]
        return dot_nt(flat.astype(jnp.bfloat16), q[layer])

    from_peers(u_recv, u_ss, u_rs)
    from_peers(vk_recv, vk_ss, vk_rs)
    u_kv, u_o = u_send[z, 0], u_send[z, 1]
    for p in tp_peers():
        u_kv = u_kv + u_recv[p, 0]
        u_o = u_o + u_recv[p, 1]
        vkv = vkv + vk_recv[p].astype(jnp.float32)
    u_kv = u_kv * inv
    q_l.wait()

    def p_take(s_, total):
        remote(p_recv.at[s_], p_recv.at[s_], p_ss.at[s_], p_rs.at[s_], s_, z).wait_recv()
        return total + p_recv[s_].astype(jnp.float32)

    vo = lax.fori_loop(sec + 1, S, p_take, vtop[...])
    vo_send[...] = vo.astype(jnp.bfloat16)
    vo_out = to_peers(vo_send, vo_recv, vo_ss, vo_rs)
    for c in vo_out:
        c.start()
    kv_scores = layer_scores(u_kv, vkv, 0)
    from_peers(vo_recv, vo_ss, vo_rs)
    for p in tp_peers():
        vo = vo + vo_recv[p].astype(jnp.float32)
    mine = kv_scores + layer_scores(u_o, vo, 1)

    fs_send[...] = mine

    def fs_copy(o):
        s_ = lax.rem(sec + o, S)
        return remote(fs_send, fs_recv.at[sec], fs_ss.at[s_], fs_rs.at[sec], s_, z)

    def fs_take(o, total):
        s_ = lax.rem(sec + o, S)
        remote(fs_recv.at[s_], fs_recv.at[s_], fs_ss.at[s_], fs_rs.at[s_], s_, z).wait_recv()
        return total

    each(1, S, lambda o: fs_copy(o).start())
    lax.fori_loop(1, S, fs_take, 0)
    fs_recv[sec] = mine
    total = lax.fori_loop(0, S, lambda s_, t: t + fs_recv[s_], jnp.zeros_like(mine))
    ft_send[...] = total
    ft_out = to_peers(ft_send, ft_recv, ft_ss, ft_rs)
    for c in ft_out:
        c.start()
    from_peers(ft_recv, ft_ss, ft_rs)
    ft_recv[z] = total
    final = ft_recv[0]
    for j in range(1, n):
        final = final + ft_recv[j]
    out_ref[...] = final

    for c in sq_out + dt_out + u_out + vk_out + vo_out + ft_out:
        c.wait_send()
    each(1, S, lambda o: fs_copy(o).wait_send())
    each(0, sec, lambda s_: p_copy(s_).wait_send())
    each(chip + 1, S // 2, lambda c_: po_copy(c_).wait_send())
    each(0, chip, lambda c_: po_forward(c_).wait_send())

    @pl.when(core == 0)
    def _():
        po_sibling().wait_send()

    for h in range(n):
        for hf in range(2):
            @pl.when((z >= h) & (z < n - 1))
            def _():
                g_copy(z - h, h, hf, True).wait_send()

            @pl.when((z + h < n) & (z > 0))
            def _():
                g_copy(z + h, h, hf, False).wait_send()


def local(
    S, n, hidden_in, gain, w_kv, g_kv, attn, top_grad, pin_kv, pout_kv, pin_o, pout_o, queries, lengths
):
    T, d = hidden_in.shape[1:]
    kc = g_kv.shape[2]
    R = pin_kv.shape[2]
    NQ = queries.shape[2]
    E = lengths.shape[0] * lengths.shape[1]
    ri = R // n
    bf, f32 = jnp.bfloat16, jnp.float32
    V = pltpu.VMEM
    DMA = pltpu.SemaphoreType.DMA
    scratch = [
        V((T, d), bf), V((1, d), bf), V((n, d, kc), bf), V((n, T, kc), bf), V((T, d), bf), V((T, d), bf),
        V((R, d), bf), V((R, kc), bf), V((R, d), bf), V((S, R, d), bf), V(queries.shape[1:], bf),
        V((T, d), f32), V((T, d), bf), V((S * R, T), f32), V((S * R, T), f32),
        V((S, R, T), bf), V((S, R, T), bf),
        V((1, T), f32), V((n, 1, T), f32), V((1, T), f32), V((n, 1, T), f32),
        V((n, 2, ri, T), f32), V((n, 2, ri, T), f32), V((R, T), bf), V((n, R, T), bf),
        V((R, T), bf), V((n, R, T), bf), V((R, T), f32),
        V((E, NQ), f32), V((S, E, NQ), f32), V((E, NQ), f32), V((n, E, NQ), f32),
        DMA((10,)), DMA((n,)), DMA((n, 2)), DMA((n, 2)), DMA((n, 2)),
        DMA((S // 2,)), DMA, DMA((S // 2,)), DMA((S,)),
    ] + [DMA((n,))] * 10 + [DMA((S,))] * 4 + [DMA((n,))] * 2
    anywhere = pl.BlockSpec(memory_space=pl.ANY)

    def flip(p):
        return jnp.swapaxes(p[0], 0, 1)

    return pl.pallas_call(
        functools.partial(kernel, S, n),
        out_shape=jax.ShapeDtypeStruct((E, NQ), f32),
        in_specs=[anywhere] * 11 + [pl.BlockSpec(memory_space=pltpu.SMEM)],
        out_specs=pl.BlockSpec(memory_space=pltpu.VMEM),
        scratch_shapes=scratch,
        compiler_params=pltpu.CompilerParams(
            collective_id=0, has_side_effects=True, vmem_limit_bytes=48 * 1024 * 1024
        ),
    )(
        hidden_in[0], gain, w_kv[0], g_kv[0], attn[0], top_grad,
        flip(pin_kv), flip(pout_kv), flip(pin_o), flip(pout_o), queries[0], lengths,
    )


def solution(mesh):
    S, n = mesh.shape["section"], mesh.shape["tp"]
    placed = (
        P("section", None, "tp"),
        P("section", "tp"),
        P("section", "tp", None),
        P("section", None, "tp"),
        P("section", None, "tp"),
        P(None, "tp"),
        P("section", "tp", None),
        P("section", "tp", None),
        P("section", "tp", None),
        P("section", "tp", None),
        P("section", None, None, "tp"),
        P(),
    )
    return jax.shard_map(
        functools.partial(local, S, n), mesh=mesh, in_specs=placed, out_specs=P(), check_vma=False
    )
```

```python
import functools

import jax
import jax.numpy as jnp
from jax import lax
from jax.experimental import pallas as pl
from jax.experimental.pallas import tpu as pltpu
from jax.sharding import PartitionSpec as P

EPSILON = 1e-05
MESH = pl.DeviceIdType.MESH
NT = (((1,), (1,)), ((), ()))


def dot_nt(a, b):
    return lax.dot_general(a, b, NT, preferred_element_type=jnp.float32)


def fold(x):
    total = x[:, :128]
    for first in range(128, x.shape[1], 128):
        total = total + x[:, first:first + 128]
    return total


def as_row(x):
    return jnp.sum(x.T, axis=0, keepdims=True)


def kernel(
    S, n,
    hid_h, gain_h, w_h, g_h, att_h, top_h, pik_h, pok_h, pio_h, poo_h, q_h, len_s,
    out_ref,
    hid, gain, w, g, att, top, pik, pok, pio, pout, q,
    da, e, a_t, b_t, p_send, p_recv,
    sq_send, sq_recv, dt_send, dt_recv, u_send, u_recv, vk_send, vk_recv,
    vo_send, vo_recv, vtop, fs_send, fs_recv, ft_send, ft_recv,
    loc, w_sem, g_up, g_dn, g_rs, po_ss, po_sib, po_fw, po_rs,
    sq_ss, sq_rs, dt_ss, dt_rs, u_ss, u_rs, vk_ss, vk_rs, vo_ss, vo_rs,
    p_ss, p_rs, fs_ss, fs_rs, ft_ss, ft_rs,
):
    sec, z = lax.axis_index("section"), lax.axis_index("tp")
    chip, core = sec // 2, sec % 2
    sib = 2 * chip + 1 - core
    T, d = hid.shape
    kc = g.shape[2]
    R = pik.shape[0]
    ri = R // n
    D = d * n
    half = T // 2
    tile = min(d, 512)
    tiles = d // tile

    def remote(src, dst, ss, rs, s_, z_):
        return pltpu.make_async_remote_copy(
            src_ref=src, dst_ref=dst, send_sem=ss, recv_sem=rs,
            device_id={"section": s_, "tp": z_}, device_id_type=MESH,
        )

    def tp_peers():
        return [lax.rem(z + o, n) for o in range(1, n)]

    g_load = pltpu.make_async_copy(g_h, g.at[z], loc.at[0])
    po_load = pltpu.make_async_copy(poo_h, pout.at[sec], loc.at[1])
    g_load.start()
    po_load.start()
    rest = [
        pltpu.make_async_copy(src, dst, loc.at[2 + i])
        for i, (src, dst) in enumerate(
            [(hid_h, hid), (gain_h, gain), (pik_h, pik), (att_h, att), (pio_h, pio),
             (pok_h, pok), (top_h, top), (q_h, q)]
        )
    ]
    hid_l, gain_l, pik_l, att_l, pio_l, pok_l, top_l, q_l = rest
    for c in rest[:6]:
        c.start()

    def w_load(ch):
        return pltpu.make_async_copy(
            w_h.at[:, pl.ds(pl.multiple_of(ch * kc, 128), kc)], w.at[ch], w_sem.at[ch]
        )

    w_load(z).start()
    for peer in tp_peers():
        w_load(peer).start()
    top_l.start()
    q_l.start()

    barrier = pltpu.get_barrier_semaphore()
    for peer in tp_peers():
        pl.semaphore_signal(barrier, inc=1, device_id={"section": sec, "tp": peer}, device_id_type=MESH)

    def greet(o, carry):
        pl.semaphore_signal(
            barrier, inc=1, device_id={"section": lax.rem(sec + o, S), "tp": z}, device_id_type=MESH
        )
        return carry

    lax.fori_loop(1, S, greet, 0)
    pl.semaphore_wait(barrier, n - 1 + S - 1)

    def g_copy(ch, h, hf, up):
        part = g.at[ch, pl.ds(hf * half, half)]
        sems = g_up if up else g_dn
        return remote(part, part, sems.at[h, hf], g_rs.at[ch, hf], sec, z + 1 if up else z - 1)

    g_load.wait()
    for hf in range(2):
        @pl.when(z < n - 1)
        def _():
            g_copy(z, 0, hf, True).start()

        @pl.when(z > 0)
        def _():
            g_copy(z, 0, hf, False).start()

    po_load.wait()

    def po_copy(c_):
        return remote(pout.at[sec], pout.at[sec], po_ss.at[c_], po_rs.at[sec], 2 * c_ + core, z)

    def po_sibling():
        return remote(pout.at[sec], pout.at[sec], po_sib, po_rs.at[sec], sib, z)

    def po_forward(c_):
        s_ = 2 * c_ + core
        return remote(pout.at[s_], pout.at[s_], po_fw.at[c_], po_rs.at[s_], sib, z)

    def each(lo, hi, act):
        def body(i, carry):
            act(i)
            return carry
        lax.fori_loop(lo, hi, body, 0)

    each(chip + 1, S // 2, lambda c_: po_copy(c_).start())

    @pl.when(core == 0)
    def _():
        po_sibling().start()

    hid_l.wait()
    gain_l.wait()

    def cut(i):
        return pl.ds(pl.multiple_of(i * tile, 128), tile)

    def squares(i, total):
        x = hid[:, cut(i)].astype(jnp.float32)
        e[:, cut(i)] = (x * gain[:, cut(i)].astype(jnp.float32)).astype(jnp.bfloat16)
        return total + fold(x * x)

    sq_mine = as_row(lax.fori_loop(0, tiles, squares, jnp.zeros((T, 128), jnp.float32)))

    def to_peers(send, recv, ss, rs):
        return [remote(send, recv.at[z], ss.at[peer], rs.at[z], sec, peer) for peer in tp_peers()]

    def from_peers(recv, ss, rs):
        for peer in tp_peers():
            remote(recv.at[peer], recv.at[peer], ss.at[peer], rs.at[peer], sec, peer).wait_recv()

    sq_send[...] = sq_mine
    sq_out = to_peers(sq_send, sq_recv, sq_ss, sq_rs)
    for c in sq_out:
        c.start()

    pik_l.wait()
    uk = dot_nt(pik[...], e[...])
    pok_l.wait()
    vk = dot_nt(pok[...], g[z])
    att_l.wait()
    pio_l.wait()
    uo = dot_nt(pio[...], att[...])
    for j in range(n):
        u_send[j, 0] = uk[j * ri:(j + 1) * ri]
        u_send[j, 1] = uo[j * ri:(j + 1) * ri]
    vk_send[...] = vk.astype(jnp.bfloat16)
    vkv = vk

    def gather_product(ch, first=False):
        def body(i, carry):
            rows = pl.ds(pl.multiple_of(i * tile, 128), tile)
            part = dot_nt(g[ch], w[ch, rows, :])
            if first:
                da[:, cut(i)] = part
            else:
                da[:, cut(i)] += part
            return carry
        w_load(ch).wait()
        lax.fori_loop(0, tiles, body, 0)

    def b_part(group):
        width = min(S, 4)

        def body(i, carry):
            rows = pl.ds(pl.multiple_of(i * width * R, 128), width * R)
            group(rows, pout[pl.ds(i * width, width)].reshape(width * R, d))
            return carry
        lax.fori_loop(0, S // width, body, 0)

    def project_inputs(rows, po):
        b_t[rows, :] = dot_nt(po, hid[...])

    def project_grads(rows, po):
        a_t[rows, :] = dot_nt(po, e[...])

    def po_arrived(s_):
        remote(pout.at[s_], pout.at[s_], po_sib, po_rs.at[s_], sib, z).wait_recv()

    def arrive(h):
        for hf in range(2):
            @pl.when(z >= h)
            def _():
                g_copy(z - h, h, hf, True).wait_recv()

                @pl.when(z < n - 1)
                def _():
                    g_copy(z - h, h, hf, True).start()

            @pl.when(z + h < n)
            def _():
                g_copy(z + h, h, hf, False).wait_recv()

                @pl.when(z > 0)
                def _():
                    g_copy(z + h, h, hf, False).start()

    def products(h):
        if h == 0:
            gather_product(z, first=True)
            top_l.wait()
            vtop[...] = dot_nt(pout[sec], top[...])
            return

        @pl.when(z >= h)
        def _():
            gather_product(z - h)

        @pl.when(z + h < n)
        def _():
            gather_product(z + h)

    for h in range(1, n - 1):
        arrive(h)
        products(h - 1)
    products(n - 2)

    def pass_on(c_):
        po_arrived(2 * c_ + core)
        po_forward(c_).start()

    each(0, chip, pass_on)
    each(0, chip, lambda c_: po_arrived(2 * c_ + 1 - core))

    @pl.when(core == 1)
    def _():
        po_arrived(sib)

    b_part(project_inputs)
    arrive(n - 1)
    products(n - 1)

    def weigh(i, total):
        part = da[:, cut(i)] * gain[:, cut(i)].astype(jnp.float32)
        e[:, cut(i)] = part.astype(jnp.bfloat16)
        return total + fold(part * hid[:, cut(i)].astype(jnp.float32))

    dt_mine = as_row(lax.fori_loop(0, tiles, weigh, jnp.zeros((T, 128), jnp.float32)))
    dt_send[...] = dt_mine
    dt_out = to_peers(dt_send, dt_recv, dt_ss, dt_rs)
    for c in dt_out:
        c.start()
    u_out = [remote(u_send.at[p], u_recv.at[z], u_ss.at[p], u_rs.at[z], sec, p) for p in tp_peers()]
    vk_out = to_peers(vk_send, vk_recv, vk_ss, vk_rs)
    for c in u_out + vk_out:
        c.start()

    b_part(project_grads)
    from_peers(sq_recv, sq_ss, sq_rs)
    sq_total = sq_mine
    for p in tp_peers():
        sq_total = sq_total + sq_recv[p]
    inv = lax.rsqrt(sq_total / D + EPSILON)
    from_peers(dt_recv, dt_ss, dt_rs)
    dt_total = dt_mine
    for p in tp_peers():
        dt_total = dt_total + dt_recv[p]
    coef = inv * inv * inv / D * dt_total

    def p_copy(s_):
        return remote(p_send.at[s_], p_recv.at[sec], p_ss.at[s_], p_rs.at[sec], s_, z)

    def p_make(s_):
        rows = pl.ds(pl.multiple_of(s_ * R, R), R)
        p_send[s_] = (inv * a_t[rows, :] - coef * b_t[rows, :]).astype(jnp.bfloat16)
        p_copy(s_).start()

    each(0, sec, p_make)

    batches, per = len_s.shape
    E = batches * per
    row = lax.broadcasted_iota(jnp.int32, (E, T), 0)
    token = lax.broadcasted_iota(jnp.int32, (E, T), 1)
    starts = jnp.zeros((E, T), jnp.int32)
    ends = jnp.zeros((E, T), jnp.int32)
    for m in range(batches):
        at = jnp.int32(m * (T // batches))
        for k in range(per):
            starts = jnp.where(row == m * per + k, at, starts)
            at = at + len_s[m, k]
            ends = jnp.where(row == m * per + k, at, ends)
    mask = jnp.where((token >= starts) & (token < ends), 1.0, 0.0).astype(jnp.float32)

    def layer_scores(u, v_t, layer):
        left = jnp.concatenate([mask * u[i:i + 1] for i in range(ri)], axis=0)
        grads = lax.dot_general(
            left, jnp.concatenate([v_t, v_t], axis=0), NT,
            precision=lax.Precision.HIGHEST, preferred_element_type=jnp.float32,
        )
        low = lax.broadcasted_iota(jnp.int32, (E, 2 * R), 1) < R
        pieces = [
            jnp.where(low, grads[i * E:(i + 1) * E], grads[(i + 1) * E:(i + 2) * E])
            for i in range(0, ri, 2)
        ]
        flat = jnp.concatenate(pieces, axis=1) if len(pieces) > 1 else pieces[0]
        high = flat.astype(jnp.bfloat16)
        low_part = (flat - high.astype(jnp.float32)).astype(jnp.bfloat16)
        both = dot_nt(jnp.concatenate([high, low_part], axis=0), q[layer])
        return both[:E] + both[E:]

    from_peers(u_recv, u_ss, u_rs)
    from_peers(vk_recv, vk_ss, vk_rs)
    u_kv, u_o = u_send[z, 0], u_send[z, 1]
    for p in tp_peers():
        u_kv = u_kv + u_recv[p, 0]
        u_o = u_o + u_recv[p, 1]
        vkv = vkv + vk_recv[p].astype(jnp.float32)
    u_kv = u_kv * inv
    q_l.wait()

    def p_take(s_, total):
        remote(p_recv.at[s_], p_recv.at[s_], p_ss.at[s_], p_rs.at[s_], s_, z).wait_recv()
        return total + p_recv[s_].astype(jnp.float32)

    vo = lax.fori_loop(sec + 1, S, p_take, vtop[...])
    vo_send[...] = vo.astype(jnp.bfloat16)
    vo_out = to_peers(vo_send, vo_recv, vo_ss, vo_rs)
    for c in vo_out:
        c.start()
    kv_scores = layer_scores(u_kv, vkv, 0)
    from_peers(vo_recv, vo_ss, vo_rs)
    for p in tp_peers():
        vo = vo + vo_recv[p].astype(jnp.float32)
    mine = kv_scores + layer_scores(u_o, vo, 1)

    fs_send[...] = mine

    def fs_copy(o):
        s_ = lax.rem(sec + o, S)
        return remote(fs_send, fs_recv.at[sec], fs_ss.at[s_], fs_rs.at[sec], s_, z)

    def fs_take(o, total):
        s_ = lax.rem(sec + o, S)
        remote(fs_recv.at[s_], fs_recv.at[s_], fs_ss.at[s_], fs_rs.at[s_], s_, z).wait_recv()
        return total

    each(1, S, lambda o: fs_copy(o).start())
    lax.fori_loop(1, S, fs_take, 0)
    fs_recv[sec] = mine
    total = lax.fori_loop(0, S, lambda s_, t: t + fs_recv[s_], jnp.zeros_like(mine))
    ft_send[...] = total
    ft_out = to_peers(ft_send, ft_recv, ft_ss, ft_rs)
    for c in ft_out:
        c.start()
    from_peers(ft_recv, ft_ss, ft_rs)
    ft_recv[z] = total
    final = ft_recv[0]
    for j in range(1, n):
        final = final + ft_recv[j]
    out_ref[...] = final

    for c in sq_out + dt_out + u_out + vk_out + vo_out + ft_out:
        c.wait_send()
    each(1, S, lambda o: fs_copy(o).wait_send())
    each(0, sec, lambda s_: p_copy(s_).wait_send())
    each(chip + 1, S // 2, lambda c_: po_copy(c_).wait_send())
    each(0, chip, lambda c_: po_forward(c_).wait_send())

    @pl.when(core == 0)
    def _():
        po_sibling().wait_send()

    for h in range(n):
        for hf in range(2):
            @pl.when((z >= h) & (z < n - 1))
            def _():
                g_copy(z - h, h, hf, True).wait_send()

            @pl.when((z + h < n) & (z > 0))
            def _():
                g_copy(z + h, h, hf, False).wait_send()


def local(
    S, n, hidden_in, gain, w_kv, g_kv, attn, top_grad, pin_kv, pout_kv, pin_o, pout_o, queries, lengths
):
    T, d = hidden_in.shape[1:]
    kc = g_kv.shape[2]
    R = pin_kv.shape[2]
    NQ = queries.shape[2]
    E = lengths.shape[0] * lengths.shape[1]
    ri = R // n
    bf, f32 = jnp.bfloat16, jnp.float32
    V = pltpu.VMEM
    DMA = pltpu.SemaphoreType.DMA
    scratch = [
        V((T, d), bf), V((1, d), bf), V((n, d, kc), bf), V((n, T, kc), bf), V((T, d), bf), V((T, d), bf),
        V((R, d), bf), V((R, kc), bf), V((R, d), bf), V((S, R, d), bf), V(queries.shape[1:], bf),
        V((T, d), f32), V((T, d), bf), V((S * R, T), f32), V((S * R, T), f32),
        V((S, R, T), bf), V((S, R, T), bf),
        V((1, T), f32), V((n, 1, T), f32), V((1, T), f32), V((n, 1, T), f32),
        V((n, 2, ri, T), f32), V((n, 2, ri, T), f32), V((R, T), bf), V((n, R, T), bf),
        V((R, T), bf), V((n, R, T), bf), V((R, T), f32),
        V((E, NQ), f32), V((S, E, NQ), f32), V((E, NQ), f32), V((n, E, NQ), f32),
        DMA((10,)), DMA((n,)), DMA((n, 2)), DMA((n, 2)), DMA((n, 2)),
        DMA((S // 2,)), DMA, DMA((S // 2,)), DMA((S,)),
    ] + [DMA((n,))] * 10 + [DMA((S,))] * 4 + [DMA((n,))] * 2
    anywhere = pl.BlockSpec(memory_space=pltpu.HBM)

    def flip(p):
        return jnp.swapaxes(p[0], 0, 1)

    return pl.pallas_call(
        functools.partial(kernel, S, n),
        out_shape=jax.ShapeDtypeStruct((E, NQ), f32),
        in_specs=[anywhere] * 11 + [pl.BlockSpec(memory_space=pltpu.SMEM)],
        out_specs=pl.BlockSpec(memory_space=pltpu.VMEM),
        scratch_shapes=scratch,
        compiler_params=pltpu.CompilerParams(
            collective_id=0, has_side_effects=True, vmem_limit_bytes=62 * 1024 * 1024
        ),
    )(
        hidden_in[0], gain, w_kv[0], g_kv[0], attn[0], top_grad,
        flip(pin_kv), flip(pout_kv), flip(pin_o), flip(pout_o), queries[0], lengths,
    )


def solution(mesh):
    S, n = mesh.shape["section"], mesh.shape["tp"]
    placed = (
        P("section", None, "tp"),
        P("section", "tp"),
        P("section", "tp", None),
        P("section", None, "tp"),
        P("section", None, "tp"),
        P(None, "tp"),
        P("section", "tp", None),
        P("section", "tp", None),
        P("section", "tp", None),
        P("section", "tp", None),
        P("section", None, None, "tp"),
        P(),
    )
    return jax.shard_map(
        functools.partial(local, S, n), mesh=mesh, in_specs=placed, out_specs=P(), check_vma=False
    )
```
